32 devices in a mesh: groups: 2 (over y), expert: 4 (over z), dp: 2 (over x), mp: 2 (over core).
Axes of the slice: x: 2, y: 2, z: 4, core: 2. Of those that a mesh axis runs over, the one named last changes fastest.
Arguments:
- latent: float32 [512, 2048], P(('groups', 'expert', 'dp', 'mp')), parts along dimension 0, may hold values from -6 to 6
- time_embedding: float32 [2048], replicated, may hold values from -6 to 6
- norm_gain: float32 [2, 2048], replicated, may hold values from 0.1 to 1.9
- router: float32 [2, 2048, 16], replicated, may hold values from -0.03125 to 0.03125
- up_proj: bfloat16 [2, 16, 2048, 1408], P(None, 'expert', None, 'dp'), may hold values from -0.125 to 0.125
- down_proj: bfloat16 [2, 16, 1408, 2048], P(None, 'expert', 'dp'), may hold values from -0.15625 to 0.15625
- routes: int32 [2, 2, 512, 2], P(None, None, ('groups', 'expert', 'dp', 'mp')), parts along dimension 2, may hold values from 0 to 15, all different within a row; in each aligned block of 16 rows (0 to 15, 16 to 31, ..., all dimensions but the last counted through in order) at most 2 rows name the same one
Outputs:
- next_latent: float32 [512, 2048], P(('groups', 'expert', 'dp', 'mp')), parts along dimension 0
- mean_velocity: float32 [512, 2048], P(('groups', 'expert', 'dp', 'mp')), parts along dimension 0
The draws below stay inside these ranges and needn't reach their ends.
There are 2 independent parts, one for each index of `groups`. The reference program is written for one: setup_inputs(seed, part) draws one part's arguments, and reference() takes and returns one part's arrays. A program takes and returns all parts, laid end to end along the dimension named above; an argument that names none is the same for every part. Nothing has to cross between parts.
Inputs may be any that keep to these rules, and one draw needn't show every extreme that they name: `routes`: in each evaluation and layer, the 16 tokens of one device (aligned blocks along the token dimension) name any one expert at most 2 times, a bound that some block reaches by one device's tokens; a token's two experts differ.
All inputs are finite; a program needn't handle non-finite values.
Results may differ from the reference program's by a relative error of at most 0.0055.
Values may be sent and summed in bfloat16 or wider, within the bound.
A program may use at most 128 MiB of HBM per device.

```python
import math
import jax
import jax.numpy as jnp
import numpy as np
from jax import lax

D = 2048
FF = 1408
EXPERTS = 16
TOP = 2
LAYERS = 2
TOK_DEV = 16
CAP = 2
TOKENS = 256
N_DP = 2


def shard_levels(stream_key, dims, shards, low, largest):
    def one(dim, blocks):
        draws = jax.random.uniform(jax.random.fold_in(jax.random.fold_in(stream_key, 6), dim), (blocks,), jnp.float32, low / len(shards), largest / len(shards))
        return jnp.repeat(jnp.exp(draws), dims[dim] // blocks).reshape((-1,) + (1,) * (len(dims) - dim - 1))

    loudness = one(*shards[0])
    for cut in shards[1:]:
        loudness = loudness * one(*cut)
    return loudness


def shared_out(stream_key, own, number, rows, amount, top, most, slope):
    sequence = jax.random.permutation(stream_key, amount)
    packed, ordinary = shares(amount, rows * top, most, slope, True), shares(amount, rows * top, most, slope, False)
    places = jnp.arange(amount)

    def named(sizes, turn):
        used = int((sizes > 0).sum())
        fixed = max(1, used // 4)
        moved = fixed + (places - fixed + turn * (used - fixed)) % max(1, amount - fixed)
        return jnp.zeros((amount,), jnp.int32).at[sequence[jnp.where(places < fixed, places, moved)]].set(jnp.asarray(sizes, jnp.int32))

    sizes = jnp.where(number % 4 == 0, named(packed, number // 4), named(ordinary, number - number // 4 - 1))
    mixed = jax.random.permutation(jax.random.fold_in(own, 3), amount)
    donor, receiver = mixed[0:amount // 2 * 2:2], mixed[1:amount // 2 * 2:2]
    room = jnp.minimum(sizes[donor] - 1, most - sizes[receiver]) // 2
    room = jnp.where((donor == sequence[0]) | (receiver == sequence[0]) | (sizes[receiver] == 0), 0, jnp.maximum(room, 0))
    moved = jax.random.randint(jax.random.fold_in(own, 4), (amount // 2,), 0, 1 << 20) % (room + 1)
    sizes = sizes.at[donor].add(-moved).at[receiver].add(moved)
    labels = jnp.searchsorted(jnp.cumsum(sizes), jnp.arange(rows * top), side="right").astype(jnp.int32)
    listing = labels.reshape(top, rows).T
    listing = listing[jax.random.permutation(jax.random.fold_in(own, 1), rows)]
    turn = jax.random.randint(jax.random.fold_in(own, 2), (rows, 1), 0, top)
    return jnp.take_along_axis(listing, (jnp.arange(top)[None, :] + turn) % top, axis=1)


def shares(count, total, limit, skew, full):
    portions = [(1 << 20) // math.isqrt(rank ** skew) + 1 for rank in range(1, count + 1)]
    largest = limit if full else min(limit, max(-(-total // count), total * portions[0] // sum(portions)))
    least = 1 if total - largest >= count - 1 else 0
    given, rest = [largest] + [least] * (count - 1), total - largest - least * (count - 1)
    while rest > 0:
        free = [i for i in range(1, count) if given[i] < largest] or [i for i in range(1, count) if given[i] < limit]
        mass, left = sum([portions[i] for i in free]), rest
        for i in free:
            more = min(limit - given[i], max(1, left * portions[i] // mass), rest)
            given[i] = given[i] + more
            rest = rest - more
    return np.array(given)


def noise(rng, extent, width, most, split=(), held_as=jnp.bfloat16):
    result = jax.random.normal(rng, extent, jnp.float32) * width
    if len(split) > 0:
        result = shard_levels(rng, extent, split, -0.22, 0.18) * result
    return jnp.clip(result, min=-most, max=most).astype(held_as)


def setup_inputs(seed: int = 0, part: int = 0) -> dict:
    keys = jax.random.split(jax.random.key(seed), 8)
    part_keys = jax.random.split(jax.random.fold_in(keys[7], part), 8)
    latent = noise(part_keys[0], (TOKENS, D), 1.0, 6.0, ((0, 16),), jnp.float32)
    time_embedding = noise(keys[1], (D,), 1.0, 6.0, (), jnp.float32)
    norm_gain = jnp.clip(1.0 + 0.18 * jax.random.normal(keys[2], (LAYERS, D), jnp.float32), 0.1, 1.9)
    router = noise(keys[3], (LAYERS, D, EXPERTS), (16 * D) ** -0.5, 0.03125, (), jnp.float32)
    up_proj = noise(keys[4], (LAYERS, EXPERTS, D, FF), D ** -0.5, 0.125, ((1, 4), (3, 2)))
    down_proj = noise(keys[5], (LAYERS, EXPERTS, FF, D), FF ** -0.5, 0.15625, ((1, 4), (2, 2)))
    routes_keys = jax.random.split(jax.random.fold_in(part_keys[6], 1), 2 * LAYERS * TOKENS // TOK_DEV)
    routes_turns = jax.random.permutation(jax.random.fold_in(part_keys[6], 3), 2 * LAYERS * TOKENS // TOK_DEV)
    routes = jax.vmap(lambda own, number: shared_out(jax.random.fold_in(part_keys[6], 2), own, number, TOK_DEV, EXPERTS, TOP, CAP, 2))(routes_keys, routes_turns).reshape((2, LAYERS, TOKENS, TOP))
    return {"latent": latent, "time_embedding": time_embedding, "norm_gain": norm_gain, "router": router, "up_proj": up_proj, "down_proj": down_proj, "routes": routes}


epsilon = 1e-06
start_time = 1.0
step_size = -0.5

def mix_weights(scaled, router_layer, chosen):
    logits = jnp.dot(scaled, router_layer, precision=lax.Precision.HIGHEST)
    picked = jnp.take_along_axis(logits, chosen, axis=1)
    leading = jax.nn.sigmoid(picked[:, 0] - picked[:, 1])
    return jnp.stack([leading, 1.0 - leading], axis=1)

def expert_layer(normed, chosen, up_layer, down_layer):
    blocks = TOKENS // TOK_DEV
    row_count = TOK_DEV * TOP
    flat_choice = chosen.reshape(blocks, row_count).astype(jnp.int32)
    onehot = (flat_choice[:, :, None] == jnp.arange(EXPERTS, dtype=jnp.int32)[None, None, :]).astype(jnp.int32)
    before = jnp.cumsum(onehot, axis=1) - onehot
    position = lax.optimization_barrier(jnp.sum(before * onehot, axis=2)).astype(jnp.int32)
    block_index = jnp.broadcast_to(jnp.arange(blocks, dtype=jnp.int32)[:, None], (blocks, row_count))
    token_index = (block_index * TOK_DEV + jnp.broadcast_to(jnp.arange(row_count, dtype=jnp.int32)[None, :] // TOP, (blocks, row_count))).astype(jnp.int32)
    slot_owner = jnp.full((EXPERTS, blocks, CAP), -1, dtype=jnp.int32)
    slot_owner = slot_owner.at[flat_choice, block_index, position].set(token_index)
    block_width = FF // N_DP

    def one_expert(expert_id):
        slot_index = slot_owner[expert_id].reshape(-1)
        slot_rows = jnp.where((slot_index >= 0)[:, None], normed[jnp.maximum(slot_index, 0)], jnp.zeros((), jnp.bfloat16))
        hidden = jax.nn.gelu(jnp.dot(slot_rows, up_layer[expert_id], preferred_element_type=jnp.float32), approximate=True).astype(jnp.bfloat16)
        summed = jnp.zeros((slot_rows.shape[0], D), jnp.float32)
        for block_number in range(N_DP):
            partial_value = jnp.dot(hidden[:, block_number * block_width:(block_number + 1) * block_width], down_layer[expert_id, block_number * block_width:(block_number + 1) * block_width], preferred_element_type=jnp.float32).astype(jnp.bfloat16)
            partial_value = lax.optimization_barrier(partial_value)
            summed = summed + partial_value.astype(jnp.float32)
        return summed.astype(jnp.bfloat16)
    outputs = lax.map(one_expert, jnp.arange(EXPERTS, dtype=jnp.int32))
    picked = outputs[flat_choice, (block_index * CAP + position).astype(jnp.int32)]
    return picked.reshape(TOKENS, TOP, D)

def moe_block(state, gain, router_layer, up_layer, down_layer, chosen):
    inverse = lax.rsqrt(lax.optimization_barrier(jnp.mean(state * state, axis=1, keepdims=True)) + epsilon)
    scaled = state * inverse * gain[None, :]
    normed = scaled.astype(jnp.bfloat16)
    weights = mix_weights(scaled, router_layer, chosen)
    picked = expert_layer(normed, chosen, up_layer, down_layer)
    return state + lax.optimization_barrier(jnp.sum(weights[:, :, None] * picked.astype(jnp.float32), axis=1))

def velocity(latent_now, time_now, section_routes, time_embedding, norm_gain, router, up_proj, down_proj):
    state = latent_now + time_now * time_embedding[None, :]
    for layer_index in range(LAYERS):
        state = moe_block(state, norm_gain[layer_index], router[layer_index], up_proj[layer_index], down_proj[layer_index], section_routes[layer_index])
    return state - latent_now

def reference(latent, time_embedding, norm_gain, router, up_proj, down_proj, routes):
    first = velocity(latent, start_time, routes[0], time_embedding, norm_gain, router, up_proj, down_proj)
    moved = latent + step_size * first
    second = velocity(moved, start_time + step_size, routes[1], time_embedding, norm_gain, router, up_proj, down_proj)
    mean_velocity = 0.5 * (first + second)
    return (latent + step_size * mean_velocity, mean_velocity)
```

```python
import functools
import jax
import jax.numpy as jnp
from jax import lax
from jax.experimental import pallas as pl
from jax.experimental.pallas import tpu as pltpu
from jax.sharding import PartitionSpec as P

CAP = 2


epsilon = 1e-06
start_time = 1.0
step_size = -0.5


def local_block(state, gain, router_layer, up_layer, down_layer, chosen):
    tok_count = state.shape[0]
    model_width = state.shape[1]
    top_count = chosen.shape[1]
    experts = router_layer.shape[1]
    local_experts = up_layer.shape[0]
    inverse = lax.rsqrt(jnp.mean(state * state, axis=1, keepdims=True) + epsilon)
    scaled = state * inverse * gain[None, :]
    normed = scaled.astype(jnp.bfloat16)
    logits = jnp.dot(scaled, router_layer, precision=lax.Precision.HIGHEST)
    picked = jnp.take_along_axis(logits, chosen, axis=1)
    leading = jax.nn.sigmoid(picked[:, 0] - picked[:, 1])
    weights = jnp.stack([leading, 1.0 - leading], axis=1)
    flat_choice = chosen.reshape(-1)
    onehot = (flat_choice[:, None] == jnp.arange(experts, dtype=jnp.int32)[None, :]).astype(
        jnp.int32
    )
    before = jnp.cumsum(onehot, axis=0) - onehot
    position = jnp.sum(before * onehot, axis=1)
    slot_id = flat_choice * CAP + position
    targets = slot_id.reshape(tok_count, top_count)
    select = jnp.any(
        jnp.arange(experts * CAP, dtype=jnp.int32)[:, None, None] == targets[None, :, :], axis=2
    ).astype(jnp.bfloat16)
    buffer = (
        jnp.dot(select, normed, preferred_element_type=jnp.float32)
        .astype(jnp.bfloat16)
        .reshape(experts, CAP, model_width)
    )
    landed = lax.all_to_all(buffer, "expert", split_axis=0, concat_axis=0, tiled=True)
    arrived = lax.all_gather(landed[None], "dp", axis=0, tiled=True)
    group_count = arrived.shape[0]
    source_count = arrived.shape[1] // local_experts
    grouped = (
        arrived.reshape(group_count, source_count, local_experts, CAP, model_width)
        .transpose(2, 0, 1, 3, 4)
        .reshape(local_experts, group_count * source_count * CAP, model_width)
    )
    hidden = jax.nn.gelu(
        jnp.einsum("erd,edf->erf", grouped, up_layer, preferred_element_type=jnp.float32),
        approximate=True,
    ).astype(jnp.bfloat16)
    partial_value = jnp.einsum(
        "erf,efd->erd", hidden, down_layer, preferred_element_type=jnp.float32
    ).astype(jnp.bfloat16)
    partial_value = (
        partial_value.reshape(local_experts, group_count, source_count, CAP, model_width)
        .transpose(1, 2, 0, 3, 4)
        .reshape(group_count, source_count * local_experts, CAP, model_width)
    )
    owned = lax.all_to_all(partial_value, "dp", split_axis=0, concat_axis=0, tiled=True)
    summed = jnp.sum(owned.astype(jnp.float32), axis=0).astype(jnp.bfloat16)
    returned = lax.all_to_all(summed, "expert", split_axis=0, concat_axis=0, tiled=True)
    gathered = returned.reshape(experts * CAP, model_width)[slot_id].reshape(
        tok_count, top_count, model_width
    )
    return state + jnp.sum(weights[:, :, None] * gathered.astype(jnp.float32), axis=1)


def velocity(
    latent_now, time_now, section_routes, time_embedding, norm_gain, router, up_proj, down_proj
):
    state = latent_now + time_now * time_embedding[None, :]
    for layer_index in range(norm_gain.shape[0]):
        state = local_block(
            state,
            norm_gain[layer_index],
            router[layer_index],
            up_proj[layer_index],
            down_proj[layer_index],
            section_routes[layer_index],
        )
    return state - latent_now


def per_device_general(latent, time_embedding, norm_gain, router, up_proj, down_proj, routes):
    first = velocity(
        latent, start_time, routes[0], time_embedding, norm_gain, router, up_proj, down_proj
    )
    moved = latent + step_size * first
    second = velocity(
        moved,
        start_time + step_size,
        routes[1],
        time_embedding,
        norm_gain,
        router,
        up_proj,
        down_proj,
    )
    mean_velocity = 0.5 * (first + second)
    return (latent + step_size * mean_velocity, mean_velocity)


PACK = 16
BLOCKS = PACK // CAP
MESH = pl.DeviceIdType.MESH


def kernel(
    sizes,
    latent_ref, te_ref, gain_ref, router_hbm, up_hbm, down_hbm, routes_ref,
    out_ref,
    up_v, down_v, router_v, base, state, total,
    take_first, take_second, spread, unpack, pack,
    dsend, xbuf, ybuf, yrecv, zsend, rbuf,
    w_sem, router_sem, d_send, d_recv, f_send, f_recv, y_send, y_recv, r_send, r_recv,
):
    nz, nc, layers, per_core, toks, width = sizes
    cols = width // BLOCKS
    srcs = 2 * nz * nc
    half = nz * nc
    z = lax.axis_index("expert")
    x = lax.axis_index("dp")
    c = lax.axis_index("mp")

    def weight_copies(layer, j):
        mine = c * per_core + j
        return (
            pltpu.make_async_copy(up_hbm.at[layer, mine], up_v.at[layer, j], w_sem.at[layer, j, 0]),
            pltpu.make_async_copy(
                down_hbm.at[layer, mine], down_v.at[layer, j], w_sem.at[layer, j, 1]
            ),
        )

    router_copy = pltpu.make_async_copy(router_hbm, router_v, router_sem)
    for layer in range(layers):
        for j in range(per_core):
            for copy in weight_copies(layer, j):
                copy.start()
        if layer == 0:
            router_copy.start()

    barrier = pltpu.get_barrier_semaphore()
    others = [(dz, dc) for dz in range(nz) for dc in range(nc) if (dz, dc) != (0, 0)]
    for dz, dc in others:
        pl.semaphore_signal(
            barrier, inc=1, device_id={"expert": lax.rem(z + dz, nz), "mp": lax.rem(c + dc, nc)},
            device_id_type=MESH,
        )
    pl.semaphore_signal(barrier, inc=1, device_id={"dp": 1 - x}, device_id_type=MESH)

    def places(rows, lanes, target):
        lane = lax.broadcasted_iota(jnp.int32, (rows, lanes), 1)
        return jnp.where(lane == target, 1.0, 0.0)

    rows_in = srcs * PACK
    per_block = srcs * CAP
    i = lax.broadcasted_iota(jnp.int32, (rows_in, 1), 0)
    unpack[...] = places(
        rows_in, rows_in, (i % per_block) // CAP * PACK + i // per_block * CAP + i % CAP
    ).astype(jnp.bfloat16)
    back = half * PACK
    i = lax.broadcasted_iota(jnp.int32, (back, 1), 0)
    pack[...] = places(
        back, back, (i % PACK) // CAP * (half * CAP) + i // PACK * CAP + i % CAP
    ).astype(jnp.bfloat16)
    experts = nz * nc * per_core

    def route(p, carry):
        chosen = routes_ref[p // layers, p % layers]
        first, second = chosen[:, 0:1], chosen[:, 1:2]
        lane = lax.broadcasted_iota(jnp.int32, (toks, 128), 1)
        one = jnp.where(lane == first, 1.0, 0.0)
        two = jnp.where(lane == second, 1.0, 0.0)
        earlier = jnp.where(
            lax.broadcasted_iota(jnp.int32, (toks, toks), 0)
            > lax.broadcasted_iota(jnp.int32, (toks, toks), 1), 1.0, 0.0,
        )
        position = jnp.dot(
            earlier.astype(jnp.bfloat16), (one + two).astype(jnp.bfloat16),
            preferred_element_type=jnp.float32,
        )
        at_first = first * PACK + jnp.sum(position * one, axis=1, keepdims=True).astype(jnp.int32)
        at_second = second * PACK + jnp.sum(position * two, axis=1, keepdims=True).astype(jnp.int32)
        block = lax.broadcasted_iota(jnp.int32, (BLOCKS * toks, 1), 0) // toks * CAP
        g0 = places(BLOCKS * toks, experts * PACK, jnp.concatenate([at_first] * BLOCKS, 0) + block)
        g1 = places(BLOCKS * toks, experts * PACK, jnp.concatenate([at_second] * BLOCKS, 0) + block)
        take_first[p] = g0.astype(jnp.bfloat16)
        take_second[p] = g1.astype(jnp.bfloat16)
        spread[p] = jnp.transpose(g0 + g1).astype(jnp.bfloat16)
        return carry

    lax.fori_loop(0, 2 * layers, route, 0)
    base[...] = latent_ref[...]
    pl.semaphore_wait(barrier, len(others) + 1)
    router_copy.wait()

    def dispatch_copy(j, dz, dc, src_z, src_c):
        to_z, to_c = lax.rem(src_z + dz, nz), lax.rem(src_c + dc, nc)
        expert = (to_z * nc + to_c) * per_core + j
        return pltpu.make_async_remote_copy(
            src_ref=dsend.at[pl.ds(pl.multiple_of(expert * PACK, PACK), PACK)],
            dst_ref=xbuf.at[
                j, pl.ds(pl.multiple_of(((x * nz + src_z) * nc + src_c) * PACK, PACK), PACK)
            ],
            send_sem=d_send.at[j, dz, dc],
            recv_sem=d_recv.at[j, dz, dc],
            device_id={"expert": to_z, "mp": to_c},
            device_id_type=MESH,
        )

    def forward_copy(j, dz, side):
        src_z = lax.rem(z + nz - dz, nz)
        rows = pl.ds(pl.multiple_of((side * nz + src_z) * nc * PACK, nc * PACK), nc * PACK)
        return pltpu.make_async_remote_copy(
            src_ref=xbuf.at[j, rows],
            dst_ref=xbuf.at[j, rows],
            send_sem=f_send.at[j, dz],
            recv_sem=f_recv.at[j, dz],
            device_id={"dp": 1 - x},
            device_id_type=MESH,
        )

    def result_copy(j):
        return pltpu.make_async_remote_copy(
            src_ref=ybuf.at[j, 1 - x],
            dst_ref=yrecv.at[j],
            send_sem=y_send.at[j],
            recv_sem=y_recv.at[j],
            device_id={"dp": 1 - x},
            device_id_type=MESH,
        )

    def return_copy(j, dz, dc, src_z, src_c):
        to_z, to_c = lax.rem(src_z + dz, nz), lax.rem(src_c + dc, nc)
        expert = (src_z * nc + src_c) * per_core + j
        return pltpu.make_async_remote_copy(
            src_ref=zsend.at[j, pl.ds(pl.multiple_of((to_z * nc + to_c) * PACK, PACK), PACK)],
            dst_ref=rbuf.at[pl.ds(pl.multiple_of(expert * PACK, PACK), PACK)],
            send_sem=r_send.at[j, dz, dc],
            recv_sem=r_recv.at[j, dz, dc],
            device_id={"expert": to_z, "mp": to_c},
            device_id_type=MESH,
        )

    def came_from(dz, dc):
        return lax.rem(z + nz - dz, nz), lax.rem(c + nc - dc, nc)

    def step(p, carry):
        layer = lax.rem(p, layers)
        evaluation = p // layers

        @pl.when(layer == 0)
        def _():
            now = jnp.where(evaluation == 0, start_time, start_time + step_size)
            state[...] = base[...] + now * te_ref[...]

        old = state[...]
        inverse = lax.rsqrt(jnp.mean(old * old, axis=1, keepdims=True) + epsilon)
        scaled = old * inverse * gain_ref[pl.ds(layer, 1), :]
        normed = scaled.astype(jnp.bfloat16)
        stacked = jnp.concatenate(
            [normed[:, b * cols:(b + 1) * cols] for b in range(BLOCKS)], axis=0
        )
        dsend[...] = jnp.dot(
            spread[p], stacked, preferred_element_type=jnp.float32
        ).astype(jnp.bfloat16)
        for j in range(per_core):
            for dz, dc in others:
                dispatch_copy(j, dz, dc, z, c).start()
        for j in range(per_core):
            expert = (z * nc + c) * per_core + j
            xbuf[j, pl.ds(pl.multiple_of(((x * nz + z) * nc + c) * PACK, PACK), PACK)] = dsend[
                pl.ds(pl.multiple_of(expert * PACK, PACK), PACK)
            ]

        logits = jnp.dot(
            scaled, router_v[layer], precision=lax.Precision.HIGHEST,
            preferred_element_type=jnp.float32,
        )
        chosen = routes_ref[evaluation, layer]
        lane = lax.broadcasted_iota(jnp.int32, logits.shape, 1)
        of_first = jnp.sum(jnp.where(lane == chosen[:, 0:1], logits, 0.0), axis=1, keepdims=True)
        of_second = jnp.sum(jnp.where(lane == chosen[:, 1:2], logits, 0.0), axis=1, keepdims=True)
        mix0 = jax.nn.sigmoid(of_first - of_second)
        mix1 = 1.0 - mix0

        for j in range(per_core):
            for dz in range(nz):
                for dc in range(nc):
                    if (dz, dc) != (0, 0):
                        dispatch_copy(j, dz, dc, *came_from(dz, dc)).wait_recv()
                forward_copy(j, dz, x).start()

        for j in range(per_core):
            for dz in range(nz):
                forward_copy(j, dz, 1 - x).wait_recv()

            @pl.when(evaluation == 0)
            def _():
                for copy in weight_copies(layer, j):
                    copy.wait()

            rows = jnp.dot(
                unpack[...], xbuf[j], preferred_element_type=jnp.float32
            ).astype(jnp.bfloat16)
            acc = jnp.dot(
                rows[:per_block], up_v[layer, j, :cols, :], preferred_element_type=jnp.float32
            )
            for b in range(1, BLOCKS):
                acc += jnp.dot(
                    rows[b * per_block:(b + 1) * per_block],
                    up_v[layer, j, b * cols:(b + 1) * cols, :],
                    preferred_element_type=jnp.float32,
                )
            hidden = jax.nn.gelu(acc, approximate=True).astype(jnp.bfloat16)
            out = jnp.dot(
                hidden, down_v[layer, j], preferred_element_type=jnp.float32
            ).astype(jnp.bfloat16)
            ybuf[j, 0] = out[:per_block // 2]
            ybuf[j, 1] = out[per_block // 2:]
            result_copy(j).start()

        for j in range(per_core):
            for dz in range(nz):
                forward_copy(j, dz, x).wait_send()
        for j in range(per_core):
            result_copy(j).wait_recv()
            summed = (
                ybuf[j, x].astype(jnp.float32) + yrecv[j].astype(jnp.float32)
            ).astype(jnp.bfloat16)
            tall = jnp.concatenate(
                [summed[:, b * cols:(b + 1) * cols] for b in range(BLOCKS)], axis=0
            )
            zsend[j] = jnp.dot(
                pack[...], tall, preferred_element_type=jnp.float32
            ).astype(jnp.bfloat16)
            for dz, dc in others:
                return_copy(j, dz, dc, z, c).start()
            expert = (z * nc + c) * per_core + j
            rbuf[pl.ds(pl.multiple_of(expert * PACK, PACK), PACK)] = zsend[
                j, pl.ds(pl.multiple_of((z * nc + c) * PACK, PACK), PACK)
            ]

        for j in range(per_core):
            result_copy(j).wait_send()
            for dz, dc in others:
                dispatch_copy(j, dz, dc, z, c).wait_send()
        for j in range(per_core):
            for dz, dc in others:
                return_copy(j, dz, dc, *came_from(dz, dc)).wait_recv()
        returned = rbuf[...]
        g0 = jnp.dot(take_first[p], returned, preferred_element_type=jnp.float32)
        g1 = jnp.dot(take_second[p], returned, preferred_element_type=jnp.float32)
        for b in range(BLOCKS):
            r = slice(b * toks, (b + 1) * toks)
            w = slice(b * cols, (b + 1) * cols)
            state[:, w] = old[:, w] + (mix0 * g0[r] + mix1 * g1[r])
        for j in range(per_core):
            for dz, dc in others:
                return_copy(j, dz, dc, z, c).wait_send()

        @pl.when(p == layers - 1)
        def _():
            first = state[...] - base[...]
            total[...] = first
            base[...] = base[...] + step_size * first

        return carry

    lax.fori_loop(0, 2 * layers, step, 0)
    out_ref[...] = total[...] + (state[...] - base[...])


def per_device(mesh_shape, latent, time_embedding, norm_gain, router, up_proj, down_proj, routes):
    nz, nc = mesh_shape["expert"], mesh_shape["mp"]
    layers, local_experts, width, hidden = up_proj.shape
    experts = router.shape[2]
    toks = latent.shape[0]
    fits = (
        mesh_shape["dp"] == 2
        and local_experts % nc == 0
        and local_experts * nz == experts
        and local_experts // nc <= 2
        and toks % 16 == 0
        and width % (BLOCKS * 128) == 0
        and hidden % 16 == 0
        and (nz * nc * CAP) % 16 == 0
        and routes.shape[0] == 2
    )
    if not fits:
        return per_device_general(
            latent, time_embedding, norm_gain, router, up_proj, down_proj, routes
        )
    per_core = local_experts // nc
    cols = width // BLOCKS
    srcs = 2 * nz * nc
    half = nz * nc
    bf16, f32 = jnp.bfloat16, jnp.float32
    vmem = pl.BlockSpec(memory_space=pltpu.VMEM)
    hbm = pl.BlockSpec(memory_space=pl.ANY)
    dma = pltpu.SemaphoreType.DMA
    flops = 2 * layers * per_core * srcs * CAP * width * hidden * 4
    total = pl.pallas_call(
        functools.partial(kernel, (nz, nc, layers, per_core, toks, width)),
        out_shape=jax.ShapeDtypeStruct((toks, width), f32),
        in_specs=[vmem, vmem, vmem, hbm, hbm, hbm, vmem],
        out_specs=vmem,
        scratch_shapes=[
            pltpu.VMEM((layers, per_core, width, hidden), bf16),
            pltpu.VMEM((layers, per_core, hidden, width), bf16),
            pltpu.VMEM((layers, width, experts), f32),
            pltpu.VMEM((toks, width), f32),
            pltpu.VMEM((toks, width), f32),
            pltpu.VMEM((toks, width), f32),
            pltpu.VMEM((2 * layers, BLOCKS * toks, experts * PACK), bf16),
            pltpu.VMEM((2 * layers, BLOCKS * toks, experts * PACK), bf16),
            pltpu.VMEM((2 * layers, experts * PACK, BLOCKS * toks), bf16),
            pltpu.VMEM((srcs * PACK, srcs * PACK), bf16),
            pltpu.VMEM((half * PACK, half * PACK), bf16),
            pltpu.VMEM((experts * PACK, cols), bf16),
            pltpu.VMEM((per_core, srcs * PACK, cols), bf16),
            pltpu.VMEM((per_core, 2, half * CAP, width), bf16),
            pltpu.VMEM((per_core, half * CAP, width), bf16),
            pltpu.VMEM((per_core, half * PACK, cols), bf16),
            pltpu.VMEM((experts * PACK, cols), bf16),
            dma((layers, per_core, 2)),
            dma,
            dma((per_core, nz, nc)),
            dma((per_core, nz, nc)),
            dma((per_core, nz)),
            dma((per_core, nz)),
            dma((per_core,)),
            dma((per_core,)),
            dma((per_core, nz, nc)),
            dma((per_core, nz, nc)),
        ],
        compiler_params=pltpu.CompilerParams(
            collective_id=0, has_side_effects=True, vmem_limit_bytes=56 * 1024 * 1024
        ),
        cost_estimate=pl.CostEstimate(
            flops=flops,
            bytes_accessed=layers * per_core * width * hidden * 4,
            transcendentals=0,
        ),
    )(latent, time_embedding.reshape(1, width), norm_gain, router, up_proj, down_proj, routes)
    mean_velocity = 0.5 * total
    return (latent + step_size * mean_velocity, mean_velocity)


def solution(mesh):
    placed = (
        P(("groups", "expert", "dp", "mp"), None),
        P(),
        P(),
        P(),
        P(None, "expert", None, "dp"),
        P(None, "expert", "dp", None),
        P(None, None, ("groups", "expert", "dp", "mp"), None),
    )
    return jax.shard_map(
        functools.partial(per_device, dict(mesh.shape)),
        mesh=mesh,
        in_specs=placed,
        out_specs=(
            P(("groups", "expert", "dp", "mp"), None),
            P(("groups", "expert", "dp", "mp"), None),
        ),
        check_vma=False,
    )
```

```python
import functools
import jax
import jax.numpy as jnp
from jax import lax
from jax.experimental import pallas as pl
from jax.experimental.pallas import tpu as pltpu
from jax.sharding import PartitionSpec as P

CAP = 2


epsilon = 1e-06
start_time = 1.0
step_size = -0.5


def local_block(state, gain, router_layer, up_layer, down_layer, chosen):
    tok_count = state.shape[0]
    model_width = state.shape[1]
    top_count = chosen.shape[1]
    experts = router_layer.shape[1]
    local_experts = up_layer.shape[0]
    inverse = lax.rsqrt(jnp.mean(state * state, axis=1, keepdims=True) + epsilon)
    scaled = state * inverse * gain[None, :]
    normed = scaled.astype(jnp.bfloat16)
    logits = jnp.dot(scaled, router_layer, precision=lax.Precision.HIGHEST)
    picked = jnp.take_along_axis(logits, chosen, axis=1)
    leading = jax.nn.sigmoid(picked[:, 0] - picked[:, 1])
    weights = jnp.stack([leading, 1.0 - leading], axis=1)
    flat_choice = chosen.reshape(-1)
    onehot = (flat_choice[:, None] == jnp.arange(experts, dtype=jnp.int32)[None, :]).astype(
        jnp.int32
    )
    before = jnp.cumsum(onehot, axis=0) - onehot
    position = jnp.sum(before * onehot, axis=1)
    slot_id = flat_choice * CAP + position
    targets = slot_id.reshape(tok_count, top_count)
    select = jnp.any(
        jnp.arange(experts * CAP, dtype=jnp.int32)[:, None, None] == targets[None, :, :], axis=2
    ).astype(jnp.bfloat16)
    buffer = (
        jnp.dot(select, normed, preferred_element_type=jnp.float32)
        .astype(jnp.bfloat16)
        .reshape(experts, CAP, model_width)
    )
    landed = lax.all_to_all(buffer, "expert", split_axis=0, concat_axis=0, tiled=True)
    arrived = lax.all_gather(landed[None], "dp", axis=0, tiled=True)
    group_count = arrived.shape[0]
    source_count = arrived.shape[1] // local_experts
    grouped = (
        arrived.reshape(group_count, source_count, local_experts, CAP, model_width)
        .transpose(2, 0, 1, 3, 4)
        .reshape(local_experts, group_count * source_count * CAP, model_width)
    )
    hidden = jax.nn.gelu(
        jnp.einsum("erd,edf->erf", grouped, up_layer, preferred_element_type=jnp.float32),
        approximate=True,
    ).astype(jnp.bfloat16)
    partial_value = jnp.einsum(
        "erf,efd->erd", hidden, down_layer, preferred_element_type=jnp.float32
    ).astype(jnp.bfloat16)
    partial_value = (
        partial_value.reshape(local_experts, group_count, source_count, CAP, model_width)
        .transpose(1, 2, 0, 3, 4)
        .reshape(group_count, source_count * local_experts, CAP, model_width)
    )
    owned = lax.all_to_all(partial_value, "dp", split_axis=0, concat_axis=0, tiled=True)
    summed = jnp.sum(owned.astype(jnp.float32), axis=0).astype(jnp.bfloat16)
    returned = lax.all_to_all(summed, "expert", split_axis=0, concat_axis=0, tiled=True)
    gathered = returned.reshape(experts * CAP, model_width)[slot_id].reshape(
        tok_count, top_count, model_width
    )
    return state + jnp.sum(weights[:, :, None] * gathered.astype(jnp.float32), axis=1)


def velocity(
    latent_now, time_now, section_routes, time_embedding, norm_gain, router, up_proj, down_proj
):
    state = latent_now + time_now * time_embedding[None, :]
    for layer_index in range(norm_gain.shape[0]):
        state = local_block(
            state,
            norm_gain[layer_index],
            router[layer_index],
            up_proj[layer_index],
            down_proj[layer_index],
            section_routes[layer_index],
        )
    return state - latent_now


def per_device_general(latent, time_embedding, norm_gain, router, up_proj, down_proj, routes):
    first = velocity(
        latent, start_time, routes[0], time_embedding, norm_gain, router, up_proj, down_proj
    )
    moved = latent + step_size * first
    second = velocity(
        moved,
        start_time + step_size,
        routes[1],
        time_embedding,
        norm_gain,
        router,
        up_proj,
        down_proj,
    )
    mean_velocity = 0.5 * (first + second)
    return (latent + step_size * mean_velocity, mean_velocity)


PACK = 16
BLOCKS = PACK // CAP
HALVES = 2
MESH = pl.DeviceIdType.MESH


def kernel(
    sizes,
    latent_ref, te_ref, gain_ref, router_ref, up_hbm, down_hbm, routes_ref,
    out_ref,
    up_v, down_v, router_v, base, state, total,
    take_first, take_second, spread, unpack, pack,
    dsend, xbuf, ybuf, yrecv, zsend, rbuf,
    w_sem, d_send, d_recv, n_send, n_recv, f_send, f_recv, y_send, y_recv, r_send, r_recv,
):
    nz, nc, layers, per_core, toks, width = sizes
    cols = width // BLOCKS
    srcs = 2 * nz * nc
    half = nz * nc
    part = width // HALVES
    z = lax.axis_index("expert")
    x = lax.axis_index("dp")
    c = lax.axis_index("mp")

    def weight_copies(layer, j):
        mine = c * per_core + j
        return (
            pltpu.make_async_copy(up_hbm.at[layer, mine], up_v.at[layer, j], w_sem.at[layer, j, 0]),
            pltpu.make_async_copy(
                down_hbm.at[layer, mine], down_v.at[layer, j], w_sem.at[layer, j, 1]
            ),
        )

    for layer in range(layers):
        for j in range(per_core):
            for copy in weight_copies(layer, j):
                copy.start()

    def across(place, offset):
        bit = 1
        while bit <= offset:
            if offset & bit:
                place = place + bit - 2 * bit * lax.rem(lax.div(place, bit), 2)
            bit *= 2
        return place

    barrier = pltpu.get_barrier_semaphore()
    others = [(dz, dc) for dz in range(nz - 1, -1, -1) for dc in range(nc) if (dz, dc) != (0, 0)]
    for side in (x, 1 - x):
        for dz, dc in others + [(0, 0)]:
            if side is x and (dz, dc) == (0, 0):
                continue
            pl.semaphore_signal(
                barrier, inc=1,
                device_id={"expert": across(z, dz), "dp": side, "mp": across(c, dc)},
                device_id_type=MESH,
            )

    def places(rows, lanes, target):
        lane = lax.broadcasted_iota(jnp.int32, (rows, lanes), 1)
        return jnp.where(lane == target, 1.0, 0.0)

    rows_in = srcs * PACK
    per_block = srcs * CAP
    i = lax.broadcasted_iota(jnp.int32, (rows_in, 1), 0)
    unpack[...] = places(
        rows_in, rows_in, (i % per_block) // CAP * PACK + i // per_block * CAP + i % CAP
    ).astype(jnp.bfloat16)
    back = half * PACK
    i = lax.broadcasted_iota(jnp.int32, (back, 1), 0)
    pack[...] = places(
        back, back, (i % PACK) // CAP * (half * CAP) + i // PACK * CAP + i % CAP
    ).astype(jnp.bfloat16)
    experts = nz * nc * per_core

    def columns(chosen):
        same = lax.broadcasted_iota(jnp.int32, (toks, toks), 0) == lax.broadcasted_iota(
            jnp.int32, (toks, toks), 1
        )
        chosen = chosen.astype(jnp.float32)
        return [
            jnp.sum(jnp.where(same, chosen[n:n + 1, :], 0.0), axis=1, keepdims=True).astype(jnp.int32)
            for n in range(2)
        ]

    def route(p, carry):
        first, second = columns(routes_ref[p // layers, p % layers])
        lane = lax.broadcasted_iota(jnp.int32, (toks, 128), 1)
        one = jnp.where(lane == first, 1.0, 0.0)
        two = jnp.where(lane == second, 1.0, 0.0)
        earlier = jnp.where(
            lax.broadcasted_iota(jnp.int32, (toks, toks), 0)
            > lax.broadcasted_iota(jnp.int32, (toks, toks), 1), 1.0, 0.0,
        )
        position = jnp.dot(
            earlier.astype(jnp.bfloat16), (one + two).astype(jnp.bfloat16),
            preferred_element_type=jnp.float32,
        )
        at_first = first * PACK + jnp.sum(position * one, axis=1, keepdims=True).astype(jnp.int32)
        at_second = second * PACK + jnp.sum(position * two, axis=1, keepdims=True).astype(jnp.int32)
        block = lax.broadcasted_iota(jnp.int32, (BLOCKS * toks, 1), 0) // toks * CAP
        g0 = places(BLOCKS * toks, experts * PACK, jnp.concatenate([at_first] * BLOCKS, 0) + block)
        g1 = places(BLOCKS * toks, experts * PACK, jnp.concatenate([at_second] * BLOCKS, 0) + block)
        take_first[p] = g0.astype(jnp.bfloat16)
        take_second[p] = g1.astype(jnp.bfloat16)
        spread[p] = jnp.transpose(g0 + g1).astype(jnp.bfloat16)
        return carry

    lax.fori_loop(0, 2 * layers, route, 0)
    for layer in range(layers):
        high = router_ref[layer].astype(jnp.bfloat16)
        router_v[layer, :experts] = high
        router_v[layer, experts:] = (router_ref[layer] - high.astype(jnp.float32)).astype(jnp.bfloat16)
    base[...] = latent_ref[...]
    pl.semaphore_wait(barrier, srcs - 1)

    def dispatch_copy(j, dz, dc, src_z, src_c):
        to_z, to_c = across(src_z, dz), across(src_c, dc)
        expert = (to_z * nc + to_c) * per_core + j
        return pltpu.make_async_remote_copy(
            src_ref=dsend.at[pl.ds(pl.multiple_of(expert * PACK, PACK), PACK)],
            dst_ref=xbuf.at[
                j, pl.ds(pl.multiple_of(((x * nz + src_z) * nc + src_c) * PACK, PACK), PACK)
            ],
            send_sem=d_send.at[j, dz, dc],
            recv_sem=d_recv.at[j, dz, dc],
            device_id={"expert": to_z, "mp": to_c},
            device_id_type=MESH,
        )

    def near_copy(j, dz, dc, src_x, src_z, src_c):
        to_z, to_c = across(src_z, dz), across(src_c, dc)
        expert = (to_z * nc + to_c) * per_core + j
        return pltpu.make_async_remote_copy(
            src_ref=dsend.at[pl.ds(pl.multiple_of(expert * PACK, PACK), PACK)],
            dst_ref=xbuf.at[
                j, pl.ds(pl.multiple_of(((src_x * nz + src_z) * nc + src_c) * PACK, PACK), PACK)
            ],
            send_sem=n_send.at[j, dz, dc],
            recv_sem=n_recv.at[j, dz, dc],
            device_id={"expert": to_z, "dp": 1 - src_x, "mp": to_c},
            device_id_type=MESH,
        )

    near = [(dz, dc) for dz in range(min(2, nz)) for dc in range(nc)]
    far = list(range(2, nz))

    def forward_copy(j, dz, side):
        src_z = across(z, dz)
        rows = pl.ds(pl.multiple_of((side * nz + src_z) * nc * PACK, nc * PACK), nc * PACK)
        return pltpu.make_async_remote_copy(
            src_ref=xbuf.at[j, rows],
            dst_ref=xbuf.at[j, rows],
            send_sem=f_send.at[j, dz],
            recv_sem=f_recv.at[j, dz],
            device_id={"dp": 1 - x},
            device_id_type=MESH,
        )

    def result_copy(j, h):
        return pltpu.make_async_remote_copy(
            src_ref=ybuf.at[j, h, 1 - x],
            dst_ref=yrecv.at[j, h],
            send_sem=y_send.at[j, h],
            recv_sem=y_recv.at[j, h],
            device_id={"dp": 1 - x},
            device_id_type=MESH,
        )

    def return_copy(j, dz, dc, src_z, src_c):
        to_z, to_c = across(src_z, dz), across(src_c, dc)
        expert = (src_z * nc + src_c) * per_core + j
        return pltpu.make_async_remote_copy(
            src_ref=zsend.at[j, pl.ds(pl.multiple_of((to_z * nc + to_c) * PACK, PACK), PACK)],
            dst_ref=rbuf.at[pl.ds(pl.multiple_of(expert * PACK, PACK), PACK)],
            send_sem=r_send.at[j, dz, dc],
            recv_sem=r_recv.at[j, dz, dc],
            device_id={"expert": to_z, "mp": to_c},
            device_id_type=MESH,
        )

    def came_from(dz, dc):
        return across(z, dz), across(c, dc)

    def step(p, carry):
        layer = lax.rem(p, layers)
        evaluation = p // layers

        @pl.when(layer == 0)
        def _():
            now = jnp.where(evaluation == 0, start_time, start_time + step_size)
            state[...] = base[...] + now * te_ref[...]

        old = state[...]
        inverse = lax.rsqrt(jnp.mean(old * old, axis=1, keepdims=True) + epsilon)
        scaled = old * inverse * gain_ref[pl.ds(layer, 1), :]
        normed = scaled.astype(jnp.bfloat16)
        stacked = jnp.concatenate(
            [normed[:, b * cols:(b + 1) * cols] for b in range(BLOCKS)], axis=0
        )
        dsend[...] = jnp.dot(
            spread[p], stacked, preferred_element_type=jnp.float32
        ).astype(jnp.bfloat16)
        for j in range(per_core):
            for dz, dc in others:
                dispatch_copy(j, dz, dc, z, c).start()
            for dz, dc in reversed(near):
                near_copy(j, dz, dc, x, z, c).start()
        for j in range(per_core):
            expert = (z * nc + c) * per_core + j
            xbuf[j, pl.ds(pl.multiple_of(((x * nz + z) * nc + c) * PACK, PACK), PACK)] = dsend[
                pl.ds(pl.multiple_of(expert * PACK, PACK), PACK)
            ]

        low = (scaled - normed.astype(jnp.float32)).astype(jnp.bfloat16)
        parts = lax.dot_general(
            jnp.concatenate([normed, low], axis=0), router_v[layer], (((1,), (1,)), ((), ())),
            preferred_element_type=jnp.float32,
        )
        logits = parts[:toks] + parts[toks:]
        first, second = columns(routes_ref[evaluation, layer])
        lane = lax.rem(lax.broadcasted_iota(jnp.int32, logits.shape, 1), experts)
        of_first = jnp.sum(jnp.where(lane == first, logits, 0.0), axis=1, keepdims=True)
        of_second = jnp.sum(jnp.where(lane == second, logits, 0.0), axis=1, keepdims=True)
        mix0 = jax.nn.sigmoid(of_first - of_second)
        mix1 = 1.0 - mix0

        for j in range(per_core):
            for dz in far:
                for dc in range(nc):
                    dispatch_copy(j, dz, dc, *came_from(dz, dc)).wait_recv()
                forward_copy(j, dz, x).start()

        for j in range(per_core):
            for dz, dc in near:
                if (dz, dc) != (0, 0):
                    dispatch_copy(j, dz, dc, *came_from(dz, dc)).wait_recv()
                near_copy(j, dz, dc, 1 - x, *came_from(dz, dc)).wait_recv()
            for dz in far:
                forward_copy(j, dz, 1 - x).wait_recv()

            @pl.when(evaluation == 0)
            def _():
                for copy in weight_copies(layer, j):
                    copy.wait()

            rows = jnp.dot(
                unpack[...], xbuf[j], preferred_element_type=jnp.float32
            ).astype(jnp.bfloat16)
            wide = jnp.concatenate(
                [rows[b * per_block:(b + 1) * per_block] for b in range(BLOCKS)], axis=1
            )
            acc = lax.dot_general(
                wide, up_v[layer, j], (((1,), (1,)), ((), ())), preferred_element_type=jnp.float32
            )
            hidden = jax.nn.gelu(acc, approximate=True).astype(jnp.bfloat16)
            for h in range(HALVES):
                out = jnp.dot(
                    hidden, down_v[layer, j, :, h * part:(h + 1) * part],
                    preferred_element_type=jnp.float32,
                ).astype(jnp.bfloat16)
                ybuf[j, h, 0] = out[:per_block // 2]
                ybuf[j, h, 1] = out[per_block // 2:]
                result_copy(j, h).start()

        for j in range(per_core):
            for dz in far:
                forward_copy(j, dz, x).wait_send()
        for j in range(per_core):
            pieces = []
            for h in range(HALVES):
                result_copy(j, h).wait_recv()
                summed = (
                    ybuf[j, h, x].astype(jnp.float32) + yrecv[j, h].astype(jnp.float32)
                ).astype(jnp.bfloat16)
                pieces += [summed[:, b * cols:(b + 1) * cols] for b in range(BLOCKS // HALVES)]
            tall = jnp.concatenate(pieces, axis=0)
            zsend[j] = jnp.dot(
                pack[...], tall, preferred_element_type=jnp.float32
            ).astype(jnp.bfloat16)
            for dz, dc in others:
                return_copy(j, dz, dc, z, c).start()
            expert = (z * nc + c) * per_core + j
            rbuf[pl.ds(pl.multiple_of(expert * PACK, PACK), PACK)] = zsend[
                j, pl.ds(pl.multiple_of((z * nc + c) * PACK, PACK), PACK)
            ]

        for j in range(per_core):
            for h in range(HALVES):
                result_copy(j, h).wait_send()
            for dz, dc in others:
                dispatch_copy(j, dz, dc, z, c).wait_send()
            for dz, dc in near:
                near_copy(j, dz, dc, x, z, c).wait_send()
        for j in range(per_core):
            for dz, dc in others:
                return_copy(j, dz, dc, *came_from(dz, dc)).wait_recv()
        returned = rbuf[...]
        g0 = jnp.dot(take_first[p], returned, preferred_element_type=jnp.float32)
        g1 = jnp.dot(take_second[p], returned, preferred_element_type=jnp.float32)
        for b in range(BLOCKS):
            r = slice(b * toks, (b + 1) * toks)
            w = slice(b * cols, (b + 1) * cols)
            state[:, w] = old[:, w] + (mix0 * g0[r] + mix1 * g1[r])
        for j in range(per_core):
            for dz, dc in others:
                return_copy(j, dz, dc, z, c).wait_send()

        @pl.when(p == layers - 1)
        def _():
            first = state[...] - base[...]
            total[...] = first
            base[...] = base[...] + step_size * first

        return carry

    lax.fori_loop(0, 2 * layers, step, 0)
    out_ref[...] = total[...] + (state[...] - base[...])


def per_device(mesh_shape, latent, time_embedding, norm_gain, router, up_proj, down_proj, routes):
    nz, nc = mesh_shape["expert"], mesh_shape["mp"]
    layers, local_experts, width, hidden = up_proj.shape
    experts = router.shape[2]
    toks = latent.shape[0]
    fits = (
        mesh_shape["dp"] == 2
        and local_experts % nc == 0
        and local_experts * nz == experts
        and local_experts // nc <= 2
        and nz & (nz - 1) == 0
        and nc & (nc - 1) == 0
        and toks % 16 == 0
        and width % (BLOCKS * 128) == 0
        and hidden % 16 == 0
        and (nz * nc * CAP) % 16 == 0
        and routes.shape[0] == 2
    )
    if not fits:
        return per_device_general(
            latent, time_embedding, norm_gain, router, up_proj, down_proj, routes
        )
    per_core = local_experts // nc
    cols = width // BLOCKS
    srcs = 2 * nz * nc
    half = nz * nc
    bf16, f32 = jnp.bfloat16, jnp.float32
    vmem = pl.BlockSpec(memory_space=pltpu.VMEM)
    hbm = pl.BlockSpec(memory_space=pl.ANY)
    dma = pltpu.SemaphoreType.DMA
    flops = 2 * layers * per_core * srcs * CAP * width * hidden * 4
    total = pl.pallas_call(
        functools.partial(kernel, (nz, nc, layers, per_core, toks, width)),
        out_shape=jax.ShapeDtypeStruct((toks, width), f32),
        in_specs=[vmem, vmem, vmem, vmem, hbm, hbm, vmem],
        out_specs=vmem,
        scratch_shapes=[
            pltpu.VMEM((layers, per_core, hidden, width), bf16),
            pltpu.VMEM((layers, per_core, hidden, width), bf16),
            pltpu.VMEM((layers, 2 * experts, width), bf16),
            pltpu.VMEM((toks, width), f32),
            pltpu.VMEM((toks, width), f32),
            pltpu.VMEM((toks, width), f32),
            pltpu.VMEM((2 * layers, BLOCKS * toks, experts * PACK), bf16),
            pltpu.VMEM((2 * layers, BLOCKS * toks, experts * PACK), bf16),
            pltpu.VMEM((2 * layers, experts * PACK, BLOCKS * toks), bf16),
            pltpu.VMEM((srcs * PACK, srcs * PACK), bf16),
            pltpu.VMEM((half * PACK, half * PACK), bf16),
            pltpu.VMEM((experts * PACK, cols), bf16),
            pltpu.VMEM((per_core, srcs * PACK, cols), bf16),
            pltpu.VMEM((per_core, HALVES, 2, half * CAP, width // HALVES), bf16),
            pltpu.VMEM((per_core, HALVES, half * CAP, width // HALVES), bf16),
            pltpu.VMEM((per_core, half * PACK, cols), bf16),
            pltpu.VMEM((experts * PACK, cols), bf16),
            dma((layers, per_core, 2)),
            dma((per_core, nz, nc)),
            dma((per_core, nz, nc)),
            dma((per_core, nz, nc)),
            dma((per_core, nz, nc)),
            dma((per_core, nz)),
            dma((per_core, nz)),
            dma((per_core, HALVES)),
            dma((per_core, HALVES)),
            dma((per_core, nz, nc)),
            dma((per_core, nz, nc)),
        ],
        compiler_params=pltpu.CompilerParams(
            collective_id=0, has_side_effects=True, vmem_limit_bytes=56 * 1024 * 1024
        ),
        cost_estimate=pl.CostEstimate(
            flops=flops,
            bytes_accessed=layers * per_core * width * hidden * 4,
            transcendentals=0,
        ),
    )(
        latent, time_embedding.reshape(1, width), norm_gain, jnp.swapaxes(router, 1, 2),
        jnp.swapaxes(up_proj, 2, 3), down_proj, jnp.swapaxes(routes, 2, 3),
    )
    mean_velocity = 0.5 * total
    return (latent + step_size * mean_velocity, mean_velocity)


def solution(mesh):
    placed = (
        P(("groups", "expert", "dp", "mp"), None),
        P(),
        P(),
        P(),
        P(None, "expert", None, "dp"),
        P(None, "expert", "dp", None),
        P(None, None, ("groups", "expert", "dp", "mp"), None),
    )
    return jax.shard_map(
        functools.partial(per_device, dict(mesh.shape)),
        mesh=mesh,
        in_specs=placed,
        out_specs=(
            P(("groups", "expert", "dp", "mp"), None),
            P(("groups", "expert", "dp", "mp"), None),
        ),
        check_vma=False,
    )
```

```python
import functools
import jax
import jax.numpy as jnp
from jax import lax
from jax.experimental import pallas as pl
from jax.experimental.pallas import tpu as pltpu
from jax.sharding import PartitionSpec as P

CAP = 2


epsilon = 1e-06
start_time = 1.0
step_size = -0.5


def local_block(state, gain, router_layer, up_layer, down_layer, chosen):
    tok_count = state.shape[0]
    model_width = state.shape[1]
    top_count = chosen.shape[1]
    experts = router_layer.shape[1]
    local_experts = up_layer.shape[0]
    inverse = lax.rsqrt(jnp.mean(state * state, axis=1, keepdims=True) + epsilon)
    scaled = state * inverse * gain[None, :]
    normed = scaled.astype(jnp.bfloat16)
    logits = jnp.dot(scaled, router_layer, precision=lax.Precision.HIGHEST)
    picked = jnp.take_along_axis(logits, chosen, axis=1)
    leading = jax.nn.sigmoid(picked[:, 0] - picked[:, 1])
    weights = jnp.stack([leading, 1.0 - leading], axis=1)
    flat_choice = chosen.reshape(-1)
    onehot = (flat_choice[:, None] == jnp.arange(experts, dtype=jnp.int32)[None, :]).astype(
        jnp.int32
    )
    before = jnp.cumsum(onehot, axis=0) - onehot
    position = jnp.sum(before * onehot, axis=1)
    slot_id = flat_choice * CAP + position
    targets = slot_id.reshape(tok_count, top_count)
    select = jnp.any(
        jnp.arange(experts * CAP, dtype=jnp.int32)[:, None, None] == targets[None, :, :], axis=2
    ).astype(jnp.bfloat16)
    buffer = (
        jnp.dot(select, normed, preferred_element_type=jnp.float32)
        .astype(jnp.bfloat16)
        .reshape(experts, CAP, model_width)
    )
    landed = lax.all_to_all(buffer, "expert", split_axis=0, concat_axis=0, tiled=True)
    arrived = lax.all_gather(landed[None], "dp", axis=0, tiled=True)
    group_count = arrived.shape[0]
    source_count = arrived.shape[1] // local_experts
    grouped = (
        arrived.reshape(group_count, source_count, local_experts, CAP, model_width)
        .transpose(2, 0, 1, 3, 4)
        .reshape(local_experts, group_count * source_count * CAP, model_width)
    )
    hidden = jax.nn.gelu(
        jnp.einsum("erd,edf->erf", grouped, up_layer, preferred_element_type=jnp.float32),
        approximate=True,
    ).astype(jnp.bfloat16)
    partial_value = jnp.einsum(
        "erf,efd->erd", hidden, down_layer, preferred_element_type=jnp.float32
    ).astype(jnp.bfloat16)
    partial_value = (
        partial_value.reshape(local_experts, group_count, source_count, CAP, model_width)
        .transpose(1, 2, 0, 3, 4)
        .reshape(group_count, source_count * local_experts, CAP, model_width)
    )
    owned = lax.all_to_all(partial_value, "dp", split_axis=0, concat_axis=0, tiled=True)
    summed = jnp.sum(owned.astype(jnp.float32), axis=0).astype(jnp.bfloat16)
    returned = lax.all_to_all(summed, "expert", split_axis=0, concat_axis=0, tiled=True)
    gathered = returned.reshape(experts * CAP, model_width)[slot_id].reshape(
        tok_count, top_count, model_width
    )
    return state + jnp.sum(weights[:, :, None] * gathered.astype(jnp.float32), axis=1)


def velocity(
    latent_now, time_now, section_routes, time_embedding, norm_gain, router, up_proj, down_proj
):
    state = latent_now + time_now * time_embedding[None, :]
    for layer_index in range(norm_gain.shape[0]):
        state = local_block(
            state,
            norm_gain[layer_index],
            router[layer_index],
            up_proj[layer_index],
            down_proj[layer_index],
            section_routes[layer_index],
        )
    return state - latent_now


def per_device_general(latent, time_embedding, norm_gain, router, up_proj, down_proj, routes):
    first = velocity(
        latent, start_time, routes[0], time_embedding, norm_gain, router, up_proj, down_proj
    )
    moved = latent + step_size * first
    second = velocity(
        moved,
        start_time + step_size,
        routes[1],
        time_embedding,
        norm_gain,
        router,
        up_proj,
        down_proj,
    )
    mean_velocity = 0.5 * (first + second)
    return (latent + step_size * mean_velocity, mean_velocity)


PACK = 16
BLOCKS = PACK // CAP
MESH = pl.DeviceIdType.MESH


def kernel(
    sizes,
    latent_ref, te_ref, gain_ref, router_ref, up_hbm, down_hbm, routes_ref,
    out_ref,
    up_v, down_v, router_v, base, state, total,
    take_first, take_second, spread, unpack, pack,
    dsend, xbuf, pbuf, yrecv, zsend, rbuf,
    w_sem, d_send, d_recv, n_send, n_recv, f_send, f_recv, y_send, y_recv, r_send, r_recv,
    b_send, b_recv,
):
    nz, nc, layers, per_core, toks, width = sizes
    cols = width // BLOCKS
    srcs = 2 * nz * nc
    half = nz * nc
    z = lax.axis_index("expert")
    x = lax.axis_index("dp")
    c = lax.axis_index("mp")

    def weight_copies(layer, j):
        mine = c * per_core + j
        return (
            pltpu.make_async_copy(up_hbm.at[layer, mine], up_v.at[layer, j], w_sem.at[layer, j, 0]),
            pltpu.make_async_copy(
                down_hbm.at[layer, mine], down_v.at[layer, j], w_sem.at[layer, j, 1]
            ),
        )

    for layer in range(layers):
        for j in range(per_core):
            for copy in weight_copies(layer, j):
                copy.start()

    def across(place, offset):
        bit = 1
        while bit <= offset:
            if offset & bit:
                place = place + bit - 2 * bit * lax.rem(lax.div(place, bit), 2)
            bit *= 2
        return place

    rbuf[...] = jnp.zeros_like(rbuf)
    barrier = pltpu.get_barrier_semaphore()
    others = [(dz, dc) for dz in range(nz - 1, -1, -1) for dc in range(nc) if (dz, dc) != (0, 0)]
    for side in (x, 1 - x):
        for dz, dc in others + [(0, 0)]:
            if side is x and (dz, dc) == (0, 0):
                continue
            pl.semaphore_signal(
                barrier, inc=1,
                device_id={"expert": across(z, dz), "dp": side, "mp": across(c, dc)},
                device_id_type=MESH,
            )

    def places(rows, lanes, target):
        lane = lax.broadcasted_iota(jnp.int32, (rows, lanes), 1)
        return jnp.where(lane == target, 1.0, 0.0)

    rows_in = srcs * PACK
    per_block = srcs * CAP
    i = lax.broadcasted_iota(jnp.int32, (rows_in, 1), 0)
    unpack[...] = places(
        rows_in, rows_in, (i % per_block) // CAP * PACK + i // per_block * CAP + i % CAP
    ).astype(jnp.bfloat16)
    pack[...] = places(
        rows_in, rows_in, (i % PACK) // CAP * per_block + i // PACK * CAP + i % CAP
    ).astype(jnp.bfloat16)
    experts = nz * nc * per_core

    def columns(chosen):
        same = lax.broadcasted_iota(jnp.int32, (toks, toks), 0) == lax.broadcasted_iota(
            jnp.int32, (toks, toks), 1
        )
        chosen = chosen.astype(jnp.float32)
        return [
            jnp.sum(jnp.where(same, chosen[n:n + 1, :], 0.0), axis=1, keepdims=True).astype(jnp.int32)
            for n in range(2)
        ]

    def route(p, carry):
        first, second = columns(routes_ref[p // layers, p % layers])
        lane = lax.broadcasted_iota(jnp.int32, (toks, 128), 1)
        one = jnp.where(lane == first, 1.0, 0.0)
        two = jnp.where(lane == second, 1.0, 0.0)
        earlier = jnp.where(
            lax.broadcasted_iota(jnp.int32, (toks, toks), 0)
            > lax.broadcasted_iota(jnp.int32, (toks, toks), 1), 1.0, 0.0,
        )
        position = jnp.dot(
            earlier.astype(jnp.bfloat16), (one + two).astype(jnp.bfloat16),
            preferred_element_type=jnp.float32,
        )
        at_first = first * PACK + jnp.sum(position * one, axis=1, keepdims=True).astype(jnp.int32)
        at_second = second * PACK + jnp.sum(position * two, axis=1, keepdims=True).astype(jnp.int32)
        block = lax.broadcasted_iota(jnp.int32, (BLOCKS * toks, 1), 0) // toks * CAP
        g0 = places(BLOCKS * toks, experts * PACK, jnp.concatenate([at_first] * BLOCKS, 0) + block)
        g1 = places(BLOCKS * toks, experts * PACK, jnp.concatenate([at_second] * BLOCKS, 0) + block)
        take_first[p] = g0.astype(jnp.bfloat16)
        take_second[p] = g1.astype(jnp.bfloat16)
        spread[p] = jnp.transpose(g0 + g1).astype(jnp.bfloat16)
        return carry

    lax.fori_loop(0, 2 * layers, route, 0)
    for layer in range(layers):
        high = router_ref[layer].astype(jnp.bfloat16)
        router_v[layer, :experts] = high
        router_v[layer, experts:] = (router_ref[layer] - high.astype(jnp.float32)).astype(jnp.bfloat16)
    base[...] = latent_ref[...]
    pl.semaphore_wait(barrier, srcs - 1)

    near = [
        (dx, dz, dc) for dx in (1, 0) for dz in (1, 0) for dc in range(nc) if (dx, dz, dc) != (0, 0, 0)
    ]
    far = [(dz, dc) for dz in range(2, nz) for dc in range(nc)]
    far_count = (nz - 2) * nc

    def far_start(place):
        return 2 - 2 * lax.div(place, 2)

    def dispatch_copy(j, dz, dc, src_z, src_c):
        to_z, to_c = across(src_z, dz), across(src_c, dc)
        return pltpu.make_async_remote_copy(
            src_ref=dsend.at[to_z * nc + to_c, j],
            dst_ref=xbuf.at[(x * nz + src_z) * nc + src_c, j],
            send_sem=d_send.at[j, dz, dc],
            recv_sem=d_recv.at[j, dz, dc],
            device_id={"expert": to_z, "mp": to_c},
            device_id_type=MESH,
        )

    def near_copy(dx, dz, dc, src_x, src_z, src_c):
        to_x, to_z, to_c = across(src_x, dx), across(src_z, dz), across(src_c, dc)
        return pltpu.make_async_remote_copy(
            src_ref=dsend.at[to_z * nc + to_c],
            dst_ref=xbuf.at[(src_x * nz + src_z) * nc + src_c],
            send_sem=n_send.at[dx, dz, dc],
            recv_sem=n_recv.at[dx, dz, dc],
            device_id={"expert": to_z, "dp": to_x, "mp": to_c},
            device_id_type=MESH,
        )

    def forward_copy(j, dz, side):
        rows = pl.ds((side * nz + across(z, dz)) * nc, nc)
        return pltpu.make_async_remote_copy(
            src_ref=xbuf.at[rows, j],
            dst_ref=xbuf.at[rows, j],
            send_sem=f_send.at[j, dz],
            recv_sem=f_recv.at[j, dz],
            device_id={"dp": 1 - x},
            device_id_type=MESH,
        )

    def result_copy(j):
        return pltpu.make_async_remote_copy(
            src_ref=pbuf.at[pl.ds(((1 - x) * nz + far_start(z)) * nc, far_count), j],
            dst_ref=yrecv.at[j],
            send_sem=y_send.at[j],
            recv_sem=y_recv.at[j],
            device_id={"dp": 1 - x},
            device_id_type=MESH,
        )

    def return_copy(j, dz, dc, src_z, src_c):
        to_z, to_c = across(src_z, dz), across(src_c, dc)
        return pltpu.make_async_remote_copy(
            src_ref=zsend.at[j, (to_z - far_start(src_z)) * nc + to_c],
            dst_ref=rbuf.at[0, src_z * nc + src_c, j],
            send_sem=r_send.at[j, dz, dc],
            recv_sem=r_recv.at[j, dz, dc],
            device_id={"expert": to_z, "mp": to_c},
            device_id_type=MESH,
        )

    def back_copy(dx, dz, dc, src_x, src_z, src_c):
        to_x, to_z, to_c = across(src_x, dx), across(src_z, dz), across(src_c, dc)
        return pltpu.make_async_remote_copy(
            src_ref=pbuf.at[(to_x * nz + to_z) * nc + to_c],
            dst_ref=rbuf.at[dx, src_z * nc + src_c],
            send_sem=b_send.at[dx, dz, dc],
            recv_sem=b_recv.at[dx, dz, dc],
            device_id={"expert": to_z, "dp": to_x, "mp": to_c},
            device_id_type=MESH,
        )

    def near_from(dx, dz, dc):
        return across(x, dx), across(z, dz), across(c, dc)

    def came_from(dz, dc):
        return across(z, dz), across(c, dc)

    def step(p, carry):
        layer = lax.rem(p, layers)
        evaluation = p // layers

        @pl.when(layer == 0)
        def _():
            now = jnp.where(evaluation == 0, start_time, start_time + step_size)
            state[...] = base[...] + now * te_ref[...]

        old = state[...]
        inverse = lax.rsqrt(jnp.mean(old * old, axis=1, keepdims=True) + epsilon)
        scaled = old * inverse * gain_ref[pl.ds(layer, 1), :]
        normed = scaled.astype(jnp.bfloat16)
        stacked = jnp.concatenate(
            [normed[:, b * cols:(b + 1) * cols] for b in range(BLOCKS)], axis=0
        )
        dsend[...] = jnp.dot(
            spread[p], stacked, preferred_element_type=jnp.float32
        ).astype(jnp.bfloat16).reshape(dsend.shape)
        for j in range(per_core):
            for dz, dc in far:
                dispatch_copy(j, dz, dc, z, c).start()
        for offset in near:
            near_copy(*offset, x, z, c).start()
        xbuf[(x * nz + z) * nc + c] = dsend[z * nc + c]

        low = (scaled - normed.astype(jnp.float32)).astype(jnp.bfloat16)
        parts = lax.dot_general(
            jnp.concatenate([normed, low], axis=0), router_v[layer], (((1,), (1,)), ((), ())),
            preferred_element_type=jnp.float32,
        )
        logits = parts[:toks] + parts[toks:]
        first, second = columns(routes_ref[evaluation, layer])
        lane = lax.rem(lax.broadcasted_iota(jnp.int32, logits.shape, 1), experts)
        of_first = jnp.sum(jnp.where(lane == first, logits, 0.0), axis=1, keepdims=True)
        of_second = jnp.sum(jnp.where(lane == second, logits, 0.0), axis=1, keepdims=True)
        mix0 = jax.nn.sigmoid(of_first - of_second)
        mix1 = 1.0 - mix0

        for j in range(per_core):
            for dz in range(2, nz):
                for dc in range(nc):
                    dispatch_copy(j, dz, dc, *came_from(dz, dc)).wait_recv()
                forward_copy(j, dz, x).start()
        for offset in near:
            near_copy(*offset, *near_from(*offset)).wait_recv()

        for j in range(per_core):
            for dz in range(2, nz):
                forward_copy(j, dz, 1 - x).wait_recv()

            @pl.when(evaluation == 0)
            def _():
                for copy in weight_copies(layer, j):
                    copy.wait()

            rows = jnp.dot(
                unpack[...], xbuf[:, j].reshape(rows_in, cols), preferred_element_type=jnp.float32
            ).astype(jnp.bfloat16)
            wide = jnp.concatenate(
                [rows[b * per_block:(b + 1) * per_block] for b in range(BLOCKS)], axis=1
            )
            acc = lax.dot_general(
                wide, up_v[layer, j], (((1,), (1,)), ((), ())), preferred_element_type=jnp.float32
            )
            hidden = jax.nn.gelu(acc, approximate=True).astype(jnp.bfloat16)
            out = jnp.dot(
                hidden, down_v[layer, j], preferred_element_type=jnp.float32
            ).astype(jnp.bfloat16)
            tall = jnp.concatenate(
                [out[:, b * cols:(b + 1) * cols] for b in range(BLOCKS)], axis=0
            )
            pbuf[:, j] = jnp.dot(
                pack[...], tall, preferred_element_type=jnp.float32
            ).astype(jnp.bfloat16).reshape(srcs, PACK, cols)
            result_copy(j).start()

        for j in range(per_core):
            for dz in range(2, nz):
                forward_copy(j, dz, x).wait_send()
        for offset in near:
            back_copy(*offset, x, z, c).start()
        rbuf[0, z * nc + c] = pbuf[(x * nz + z) * nc + c]
        for j in range(per_core):
            result_copy(j).wait_recv()
            zsend[j] = (
                pbuf[pl.ds((x * nz + far_start(z)) * nc, far_count), j].astype(jnp.float32)
                + yrecv[j].astype(jnp.float32)
            ).astype(jnp.bfloat16)
            for dz, dc in far:
                return_copy(j, dz, dc, z, c).start()

        for j in range(per_core):
            result_copy(j).wait_send()
            for dz, dc in far:
                dispatch_copy(j, dz, dc, z, c).wait_send()
        for offset in near:
            near_copy(*offset, x, z, c).wait_send()
            back_copy(*offset, x, z, c).wait_send()
        for offset in near:
            back_copy(*offset, *near_from(*offset)).wait_recv()
        for j in range(per_core):
            for dz, dc in far:
                return_copy(j, dz, dc, *came_from(dz, dc)).wait_recv()
        mine = rbuf[0].reshape(experts * PACK, cols)
        other = rbuf[1].reshape(experts * PACK, cols)

        def taken(take):
            both = jnp.dot(take, mine, preferred_element_type=jnp.float32) + jnp.dot(
                take, other, preferred_element_type=jnp.float32
            )
            return both.astype(jnp.bfloat16).astype(jnp.float32)

        g0, g1 = taken(take_first[p]), taken(take_second[p])
        for b in range(BLOCKS):
            r = slice(b * toks, (b + 1) * toks)
            w = slice(b * cols, (b + 1) * cols)
            state[:, w] = old[:, w] + (mix0 * g0[r] + mix1 * g1[r])
        for j in range(per_core):
            for dz, dc in far:
                return_copy(j, dz, dc, z, c).wait_send()

        @pl.when(p == layers - 1)
        def _():
            first = state[...] - base[...]
            total[...] = first
            base[...] = base[...] + step_size * first

        return carry

    lax.fori_loop(0, 2 * layers, step, 0)
    out_ref[...] = total[...] + (state[...] - base[...])


def per_device(mesh_shape, latent, time_embedding, norm_gain, router, up_proj, down_proj, routes):
    nz, nc = mesh_shape["expert"], mesh_shape["mp"]
    layers, local_experts, width, hidden = up_proj.shape
    experts = router.shape[2]
    toks = latent.shape[0]
    fits = (
        mesh_shape["dp"] == 2
        and local_experts % nc == 0
        and local_experts * nz == experts
        and local_experts // nc <= 2
        and nz == 4
        and nc & (nc - 1) == 0
        and toks % 16 == 0
        and width % (BLOCKS * 128) == 0
        and hidden % 16 == 0
        and (nz * nc * CAP) % 16 == 0
        and routes.shape[0] == 2
    )
    if not fits:
        return per_device_general(
            latent, time_embedding, norm_gain, router, up_proj, down_proj, routes
        )
    per_core = local_experts // nc
    cols = width // BLOCKS
    srcs = 2 * nz * nc
    half = nz * nc
    bf16, f32 = jnp.bfloat16, jnp.float32
    vmem = pl.BlockSpec(memory_space=pltpu.VMEM)
    hbm = pl.BlockSpec(memory_space=pl.ANY)
    dma = pltpu.SemaphoreType.DMA
    flops = 2 * layers * per_core * srcs * CAP * width * hidden * 4
    total = pl.pallas_call(
        functools.partial(kernel, (nz, nc, layers, per_core, toks, width)),
        out_shape=jax.ShapeDtypeStruct((toks, width), f32),
        in_specs=[vmem, vmem, vmem, vmem, hbm, hbm, vmem],
        out_specs=vmem,
        scratch_shapes=[
            pltpu.VMEM((layers, per_core, hidden, width), bf16),
            pltpu.VMEM((layers, per_core, hidden, width), bf16),
            pltpu.VMEM((layers, 2 * experts, width), bf16),
            pltpu.VMEM((toks, width), f32),
            pltpu.VMEM((toks, width), f32),
            pltpu.VMEM((toks, width), f32),
            pltpu.VMEM((2 * layers, BLOCKS * toks, experts * PACK), bf16),
            pltpu.VMEM((2 * layers, BLOCKS * toks, experts * PACK), bf16),
            pltpu.VMEM((2 * layers, experts * PACK, BLOCKS * toks), bf16),
            pltpu.VMEM((srcs * PACK, srcs * PACK), bf16),
            pltpu.VMEM((srcs * PACK, srcs * PACK), bf16),
            pltpu.VMEM((half, per_core, PACK, cols), bf16),
            pltpu.VMEM((srcs, per_core, PACK, cols), bf16),
            pltpu.VMEM((srcs, per_core, PACK, cols), bf16),
            pltpu.VMEM((per_core, (nz - 2) * nc, PACK, cols), bf16),
            pltpu.VMEM((per_core, (nz - 2) * nc, PACK, cols), bf16),
            pltpu.VMEM((2, half, per_core, PACK, cols), bf16),
            dma((layers, per_core, 2)),
            dma((per_core, nz, nc)),
            dma((per_core, nz, nc)),
            dma((2, 2, nc)),
            dma((2, 2, nc)),
            dma((per_core, nz)),
            dma((per_core, nz)),
            dma((per_core,)),
            dma((per_core,)),
            dma((per_core, nz, nc)),
            dma((per_core, nz, nc)),
            dma((2, 2, nc)),
            dma((2, 2, nc)),
        ],
        compiler_params=pltpu.CompilerParams(
            collective_id=0, has_side_effects=True, vmem_limit_bytes=56 * 1024 * 1024
        ),
        cost_estimate=pl.CostEstimate(
            flops=flops,
            bytes_accessed=layers * per_core * width * hidden * 4,
            transcendentals=0,
        ),
    )(
        latent, time_embedding.reshape(1, width), norm_gain, jnp.swapaxes(router, 1, 2),
        jnp.swapaxes(up_proj, 2, 3), down_proj, jnp.swapaxes(routes, 2, 3),
    )
    mean_velocity = 0.5 * total
    return (latent + step_size * mean_velocity, mean_velocity)


def solution(mesh):
    placed = (
        P(("groups", "expert", "dp", "mp"), None),
        P(),
        P(),
        P(),
        P(None, "expert", None, "dp"),
        P(None, "expert", "dp", None),
        P(None, None, ("groups", "expert", "dp", "mp"), None),
    )
    return jax.shard_map(
        functools.partial(per_device, dict(mesh.shape)),
        mesh=mesh,
        in_specs=placed,
        out_specs=(
            P(("groups", "expert", "dp", "mp"), None),
            P(("groups", "expert", "dp", "mp"), None),
        ),
        check_vma=False,
    )
```

```python
import functools
import jax
import jax.numpy as jnp
from jax import lax
from jax.experimental import pallas as pl
from jax.experimental.pallas import tpu as pltpu
from jax.sharding import PartitionSpec as P

CAP = 2


epsilon = 1e-06
start_time = 1.0
step_size = -0.5


def local_block(state, gain, router_layer, up_layer, down_layer, chosen):
    tok_count = state.shape[0]
    model_width = state.shape[1]
    top_count = chosen.shape[1]
    experts = router_layer.shape[1]
    local_experts = up_layer.shape[0]
    inverse = lax.rsqrt(jnp.mean(state * state, axis=1, keepdims=True) + epsilon)
    scaled = state * inverse * gain[None, :]
    normed = scaled.astype(jnp.bfloat16)
    logits = jnp.dot(scaled, router_layer, precision=lax.Precision.HIGHEST)
    picked = jnp.take_along_axis(logits, chosen, axis=1)
    leading = jax.nn.sigmoid(picked[:, 0] - picked[:, 1])
    weights = jnp.stack([leading, 1.0 - leading], axis=1)
    flat_choice = chosen.reshape(-1)
    onehot = (flat_choice[:, None] == jnp.arange(experts, dtype=jnp.int32)[None, :]).astype(
        jnp.int32
    )
    before = jnp.cumsum(onehot, axis=0) - onehot
    position = jnp.sum(before * onehot, axis=1)
    slot_id = flat_choice * CAP + position
    targets = slot_id.reshape(tok_count, top_count)
    select = jnp.any(
        jnp.arange(experts * CAP, dtype=jnp.int32)[:, None, None] == targets[None, :, :], axis=2
    ).astype(jnp.bfloat16)
    buffer = (
        jnp.dot(select, normed, preferred_element_type=jnp.float32)
        .astype(jnp.bfloat16)
        .reshape(experts, CAP, model_width)
    )
    landed = lax.all_to_all(buffer, "expert", split_axis=0, concat_axis=0, tiled=True)
    arrived = lax.all_gather(landed[None], "dp", axis=0, tiled=True)
    group_count = arrived.shape[0]
    source_count = arrived.shape[1] // local_experts
    grouped = (
        arrived.reshape(group_count, source_count, local_experts, CAP, model_width)
        .transpose(2, 0, 1, 3, 4)
        .reshape(local_experts, group_count * source_count * CAP, model_width)
    )
    hidden = jax.nn.gelu(
        jnp.einsum("erd,edf->erf", grouped, up_layer, preferred_element_type=jnp.float32),
        approximate=True,
    ).astype(jnp.bfloat16)
    partial_value = jnp.einsum(
        "erf,efd->erd", hidden, down_layer, preferred_element_type=jnp.float32
    ).astype(jnp.bfloat16)
    partial_value = (
        partial_value.reshape(local_experts, group_count, source_count, CAP, model_width)
        .transpose(1, 2, 0, 3, 4)
        .reshape(group_count, source_count * local_experts, CAP, model_width)
    )
    owned = lax.all_to_all(partial_value, "dp", split_axis=0, concat_axis=0, tiled=True)
    summed = jnp.sum(owned.astype(jnp.float32), axis=0).astype(jnp.bfloat16)
    returned = lax.all_to_all(summed, "expert", split_axis=0, concat_axis=0, tiled=True)
    gathered = returned.reshape(experts * CAP, model_width)[slot_id].reshape(
        tok_count, top_count, model_width
    )
    return state + jnp.sum(weights[:, :, None] * gathered.astype(jnp.float32), axis=1)


def velocity(
    latent_now, time_now, section_routes, time_embedding, norm_gain, router, up_proj, down_proj
):
    state = latent_now + time_now * time_embedding[None, :]
    for layer_index in range(norm_gain.shape[0]):
        state = local_block(
            state,
            norm_gain[layer_index],
            router[layer_index],
            up_proj[layer_index],
            down_proj[layer_index],
            section_routes[layer_index],
        )
    return state - latent_now


def per_device_general(latent, time_embedding, norm_gain, router, up_proj, down_proj, routes):
    first = velocity(
        latent, start_time, routes[0], time_embedding, norm_gain, router, up_proj, down_proj
    )
    moved = latent + step_size * first
    second = velocity(
        moved,
        start_time + step_size,
        routes[1],
        time_embedding,
        norm_gain,
        router,
        up_proj,
        down_proj,
    )
    mean_velocity = 0.5 * (first + second)
    return (latent + step_size * mean_velocity, mean_velocity)


PACK = 16
BLOCKS = PACK // CAP
HALVES = 2
MESH = pl.DeviceIdType.MESH


def kernel(
    sizes,
    latent_ref, te_ref, gain_ref, router_ref, up_hbm, down_hbm, routes_ref,
    out_ref,
    up_v, down_v, router_v, base, state, total,
    take, spread, unpack, pack,
    dsend, xbuf, wide, ybuf, yrecv, zsend, rbuf,
    w_sem, d_send, d_recv, n_send, n_recv, f_send, f_recv, y_send, y_recv, r_send, r_recv,
):
    nz, nc, layers, per_core, toks, width = sizes
    cols = width // BLOCKS
    srcs = 2 * nz * nc
    half = nz * nc
    part = width // HALVES
    z = lax.axis_index("expert")
    x = lax.axis_index("dp")
    c = lax.axis_index("mp")

    def weight_copies(layer, j):
        mine = c * per_core + j
        return (
            pltpu.make_async_copy(up_hbm.at[layer, mine], up_v.at[layer, j], w_sem.at[layer, j, 0]),
            pltpu.make_async_copy(
                down_hbm.at[layer, mine], down_v.at[layer, j], w_sem.at[layer, j, 1]
            ),
        )

    for layer in range(layers):
        for j in range(per_core):
            for copy in weight_copies(layer, j):
                copy.start()

    def across(place, offset):
        bit = 1
        while bit <= offset:
            if offset & bit:
                place = place + bit - 2 * bit * lax.rem(lax.div(place, bit), 2)
            bit *= 2
        return place

    barrier = pltpu.get_barrier_semaphore()
    others = [(dz, dc) for dz in range(nz - 1, -1, -1) for dc in range(nc) if (dz, dc) != (0, 0)]
    for side in (x, 1 - x):
        for dz, dc in others + [(0, 0)]:
            if side is x and (dz, dc) == (0, 0):
                continue
            pl.semaphore_signal(
                barrier, inc=1,
                device_id={"expert": across(z, dz), "dp": side, "mp": across(c, dc)},
                device_id_type=MESH,
            )

    def places(rows, lanes, target):
        lane = lax.broadcasted_iota(jnp.int32, (rows, lanes), 1)
        return jnp.where(lane == target, 1.0, 0.0)

    per_half = half * CAP
    back = half * PACK
    i = lax.broadcasted_iota(jnp.int32, (back, 1), 0)
    unpack[...] = places(
        back, back, (i % per_half) // CAP * PACK + i // per_half * CAP + i % CAP
    ).astype(jnp.bfloat16)
    pack[...] = places(
        back, back, (i % PACK) // CAP * (half * CAP) + i // PACK * CAP + i % CAP
    ).astype(jnp.bfloat16)
    experts = nz * nc * per_core

    def columns(chosen):
        same = lax.broadcasted_iota(jnp.int32, (toks, toks), 0) == lax.broadcasted_iota(
            jnp.int32, (toks, toks), 1
        )
        chosen = chosen.astype(jnp.float32)
        return [
            jnp.sum(jnp.where(same, chosen[n:n + 1, :], 0.0), axis=1, keepdims=True).astype(jnp.int32)
            for n in range(2)
        ]

    def route(p, carry):
        first, second = columns(routes_ref[p // layers, p % layers])
        lane = lax.broadcasted_iota(jnp.int32, (toks, 128), 1)
        one = jnp.where(lane == first, 1.0, 0.0)
        two = jnp.where(lane == second, 1.0, 0.0)
        earlier = jnp.where(
            lax.broadcasted_iota(jnp.int32, (toks, toks), 0)
            > lax.broadcasted_iota(jnp.int32, (toks, toks), 1), 1.0, 0.0,
        )
        position = jnp.dot(
            earlier.astype(jnp.bfloat16), (one + two).astype(jnp.bfloat16),
            preferred_element_type=jnp.float32,
        )
        at_first = first * PACK + jnp.sum(position * one, axis=1, keepdims=True).astype(jnp.int32)
        at_second = second * PACK + jnp.sum(position * two, axis=1, keepdims=True).astype(jnp.int32)
        block = lax.broadcasted_iota(jnp.int32, (BLOCKS * toks, 1), 0) // toks * CAP
        g0 = places(BLOCKS * toks, experts * PACK, jnp.concatenate([at_first] * BLOCKS, 0) + block)
        g1 = places(BLOCKS * toks, experts * PACK, jnp.concatenate([at_second] * BLOCKS, 0) + block)
        take[p, :BLOCKS * toks] = g0.astype(jnp.bfloat16)
        take[p, BLOCKS * toks:] = g1.astype(jnp.bfloat16)
        spread[p] = jnp.transpose(g0 + g1).astype(jnp.bfloat16)
        return carry

    lax.fori_loop(0, 2 * layers, route, 0)
    for layer in range(layers):
        high = router_ref[layer].astype(jnp.bfloat16)
        router_v[layer, :experts] = high
        router_v[layer, experts:] = (router_ref[layer] - high.astype(jnp.float32)).astype(jnp.bfloat16)
    base[...] = latent_ref[...]
    pl.semaphore_wait(barrier, srcs - 1)

    def dispatch_copy(j, dz, dc, src_z, src_c):
        to_z, to_c = across(src_z, dz), across(src_c, dc)
        expert = (to_z * nc + to_c) * per_core + j
        return pltpu.make_async_remote_copy(
            src_ref=dsend.at[pl.ds(pl.multiple_of(expert * PACK, PACK), PACK)],
            dst_ref=xbuf.at[
                j, pl.ds(pl.multiple_of(((x * nz + src_z) * nc + src_c) * PACK, PACK), PACK)
            ],
            send_sem=d_send.at[j, dz, dc],
            recv_sem=d_recv.at[j, dz, dc],
            device_id={"expert": to_z, "mp": to_c},
            device_id_type=MESH,
        )

    def near_copy(j, dz, dc, src_x, src_z, src_c):
        to_z, to_c = across(src_z, dz), across(src_c, dc)
        expert = (to_z * nc + to_c) * per_core + j
        return pltpu.make_async_remote_copy(
            src_ref=dsend.at[pl.ds(pl.multiple_of(expert * PACK, PACK), PACK)],
            dst_ref=xbuf.at[
                j, pl.ds(pl.multiple_of(((src_x * nz + src_z) * nc + src_c) * PACK, PACK), PACK)
            ],
            send_sem=n_send.at[j, dz, dc],
            recv_sem=n_recv.at[j, dz, dc],
            device_id={"expert": to_z, "dp": 1 - src_x, "mp": to_c},
            device_id_type=MESH,
        )

    near = [(dz, dc) for dz in range(min(2, nz)) for dc in range(nc)]
    far = list(range(2, nz))

    def forward_copy(j, dz, side):
        src_z = across(z, dz)
        rows = pl.ds(pl.multiple_of((side * nz + src_z) * nc * PACK, nc * PACK), nc * PACK)
        return pltpu.make_async_remote_copy(
            src_ref=xbuf.at[j, rows],
            dst_ref=xbuf.at[j, rows],
            send_sem=f_send.at[j, dz],
            recv_sem=f_recv.at[j, dz],
            device_id={"dp": 1 - x},
            device_id_type=MESH,
        )

    def result_copy(j, h):
        return pltpu.make_async_remote_copy(
            src_ref=ybuf.at[j, h, 1],
            dst_ref=yrecv.at[j, h],
            send_sem=y_send.at[j, h],
            recv_sem=y_recv.at[j, h],
            device_id={"dp": 1 - x},
            device_id_type=MESH,
        )

    def return_copy(j, dz, dc, src_z, src_c):
        to_z, to_c = across(src_z, dz), across(src_c, dc)
        expert = (src_z * nc + src_c) * per_core + j
        return pltpu.make_async_remote_copy(
            src_ref=zsend.at[j, pl.ds(pl.multiple_of((to_z * nc + to_c) * PACK, PACK), PACK)],
            dst_ref=rbuf.at[pl.ds(pl.multiple_of(expert * PACK, PACK), PACK)],
            send_sem=r_send.at[j, dz, dc],
            recv_sem=r_recv.at[j, dz, dc],
            device_id={"expert": to_z, "mp": to_c},
            device_id_type=MESH,
        )

    def came_from(dz, dc):
        return across(z, dz), across(c, dc)

    def step(p, carry):
        layer = lax.rem(p, layers)
        evaluation = p // layers

        @pl.when(layer == 0)
        def _():
            now = jnp.where(evaluation == 0, start_time, start_time + step_size)
            state[...] = base[...] + now * te_ref[...]

        old = state[...]
        inverse = lax.rsqrt(jnp.mean(old * old, axis=1, keepdims=True) + epsilon)
        scaled = old * inverse * gain_ref[pl.ds(layer, 1), :]
        normed = scaled.astype(jnp.bfloat16)
        stacked = jnp.concatenate(
            [normed[:, b * cols:(b + 1) * cols] for b in range(BLOCKS)], axis=0
        )
        dsend[...] = jnp.dot(
            spread[p], stacked, preferred_element_type=jnp.float32
        ).astype(jnp.bfloat16)
        for j in range(per_core):
            for dz, dc in others:
                dispatch_copy(j, dz, dc, z, c).start()
            for dz, dc in reversed(near):
                near_copy(j, dz, dc, x, z, c).start()
        for j in range(per_core):
            expert = (z * nc + c) * per_core + j
            xbuf[j, pl.ds(pl.multiple_of(((x * nz + z) * nc + c) * PACK, PACK), PACK)] = dsend[
                pl.ds(pl.multiple_of(expert * PACK, PACK), PACK)
            ]

        low = (scaled - normed.astype(jnp.float32)).astype(jnp.bfloat16)
        parts = lax.dot_general(
            jnp.concatenate([normed, low], axis=0), router_v[layer], (((1,), (1,)), ((), ())),
            preferred_element_type=jnp.float32,
        )
        logits = parts[:toks] + parts[toks:]
        first, second = columns(routes_ref[evaluation, layer])
        lane = lax.rem(lax.broadcasted_iota(jnp.int32, logits.shape, 1), experts)
        of_first = jnp.sum(jnp.where(lane == first, logits, 0.0), axis=1, keepdims=True)
        of_second = jnp.sum(jnp.where(lane == second, logits, 0.0), axis=1, keepdims=True)
        mix0 = jax.nn.sigmoid(of_first - of_second)
        mix1 = 1.0 - mix0

        for j in range(per_core):
            for dz in far:
                for dc in range(nc):
                    dispatch_copy(j, dz, dc, *came_from(dz, dc)).wait_recv()
                forward_copy(j, dz, x).start()

        def unpacked(j, place, side):
            rows = jnp.dot(
                unpack[...], xbuf[j, pl.ds(pl.multiple_of(side * back, back), back)],
                preferred_element_type=jnp.float32,
            ).astype(jnp.bfloat16)
            for b in range(BLOCKS):
                wide[j, place * per_half:(place + 1) * per_half, b * cols:(b + 1) * cols] = rows[
                    b * per_half:(b + 1) * per_half
                ]

        for j in range(per_core):
            for dz, dc in near:
                if (dz, dc) != (0, 0):
                    dispatch_copy(j, dz, dc, *came_from(dz, dc)).wait_recv()
            unpacked(j, 0, x)

        for j in range(per_core):
            for dz, dc in near:
                near_copy(j, dz, dc, 1 - x, *came_from(dz, dc)).wait_recv()
            for dz in far:
                forward_copy(j, dz, 1 - x).wait_recv()

            @pl.when(evaluation == 0)
            def _():
                for copy in weight_copies(layer, j):
                    copy.wait()

            unpacked(j, 1, 1 - x)
            acc = lax.dot_general(
                wide[j], up_v[layer, j], (((1,), (1,)), ((), ())), preferred_element_type=jnp.float32
            )
            hidden = jax.nn.gelu(acc, approximate=True).astype(jnp.bfloat16)
            for h in range(HALVES):
                out = jnp.dot(
                    hidden, down_v[layer, j, :, h * part:(h + 1) * part],
                    preferred_element_type=jnp.float32,
                ).astype(jnp.bfloat16)
                ybuf[j, h, 0] = out[:per_half]
                ybuf[j, h, 1] = out[per_half:]
                result_copy(j, h).start()

        for j in range(per_core):
            for dz in far:
                forward_copy(j, dz, x).wait_send()
        for j in range(per_core):
            pieces = []
            for h in range(HALVES):
                result_copy(j, h).wait_recv()
                summed = (
                    ybuf[j, h, 0].astype(jnp.float32) + yrecv[j, h].astype(jnp.float32)
                ).astype(jnp.bfloat16)
                pieces += [summed[:, b * cols:(b + 1) * cols] for b in range(BLOCKS // HALVES)]
            tall = jnp.concatenate(pieces, axis=0)
            zsend[j] = jnp.dot(
                pack[...], tall, preferred_element_type=jnp.float32
            ).astype(jnp.bfloat16)
            for dz, dc in others:
                return_copy(j, dz, dc, z, c).start()
            expert = (z * nc + c) * per_core + j
            rbuf[pl.ds(pl.multiple_of(expert * PACK, PACK), PACK)] = zsend[
                j, pl.ds(pl.multiple_of((z * nc + c) * PACK, PACK), PACK)
            ]

        for j in range(per_core):
            for h in range(HALVES):
                result_copy(j, h).wait_send()
            for dz, dc in others:
                dispatch_copy(j, dz, dc, z, c).wait_send()
            for dz, dc in near:
                near_copy(j, dz, dc, x, z, c).wait_send()
        for j in range(per_core):
            for dz, dc in others:
                return_copy(j, dz, dc, *came_from(dz, dc)).wait_recv()
        returned = rbuf[...]
        both = jnp.dot(take[p], returned, preferred_element_type=jnp.float32)
        g0, g1 = both[:BLOCKS * toks], both[BLOCKS * toks:]
        for b in range(BLOCKS):
            r = slice(b * toks, (b + 1) * toks)
            w = slice(b * cols, (b + 1) * cols)
            state[:, w] = old[:, w] + (mix0 * g0[r] + mix1 * g1[r])
        for j in range(per_core):
            for dz, dc in others:
                return_copy(j, dz, dc, z, c).wait_send()

        @pl.when(p == layers - 1)
        def _():
            first = state[...] - base[...]
            total[...] = first
            base[...] = base[...] + step_size * first

        return carry

    lax.fori_loop(0, 2 * layers, step, 0)
    out_ref[...] = total[...] + (state[...] - base[...])


def per_device(mesh_shape, latent, time_embedding, norm_gain, router, up_proj, down_proj, routes):
    nz, nc = mesh_shape["expert"], mesh_shape["mp"]
    layers, local_experts, width, hidden = up_proj.shape
    experts = router.shape[2]
    toks = latent.shape[0]
    fits = (
        mesh_shape["dp"] == 2
        and local_experts % nc == 0
        and local_experts * nz == experts
        and local_experts // nc <= 2
        and nz & (nz - 1) == 0
        and nc & (nc - 1) == 0
        and toks % 16 == 0
        and width % (BLOCKS * 128) == 0
        and hidden % 16 == 0
        and (nz * nc * CAP) % 16 == 0
        and routes.shape[0] == 2
    )
    if not fits:
        return per_device_general(
            latent, time_embedding, norm_gain, router, up_proj, down_proj, routes
        )
    per_core = local_experts // nc
    cols = width // BLOCKS
    srcs = 2 * nz * nc
    half = nz * nc
    bf16, f32 = jnp.bfloat16, jnp.float32
    vmem = pl.BlockSpec(memory_space=pltpu.VMEM)
    hbm = pl.BlockSpec(memory_space=pl.ANY)
    dma = pltpu.SemaphoreType.DMA
    flops = 2 * layers * per_core * srcs * CAP * width * hidden * 4
    total = pl.pallas_call(
        functools.partial(kernel, (nz, nc, layers, per_core, toks, width)),
        out_shape=jax.ShapeDtypeStruct((toks, width), f32),
        in_specs=[vmem, vmem, vmem, vmem, hbm, hbm, vmem],
        out_specs=vmem,
        scratch_shapes=[
            pltpu.VMEM((layers, per_core, hidden, width), bf16),
            pltpu.VMEM((layers, per_core, hidden, width), bf16),
            pltpu.VMEM((layers, 2 * experts, width), bf16),
            pltpu.VMEM((toks, width), f32),
            pltpu.VMEM((toks, width), f32),
            pltpu.VMEM((toks, width), f32),
            pltpu.VMEM((2 * layers, 2 * BLOCKS * toks, experts * PACK), bf16),
            pltpu.VMEM((2 * layers, experts * PACK, BLOCKS * toks), bf16),
            pltpu.VMEM((half * PACK, half * PACK), bf16),
            pltpu.VMEM((half * PACK, half * PACK), bf16),
            pltpu.VMEM((experts * PACK, cols), bf16),
            pltpu.VMEM((per_core, srcs * PACK, cols), bf16),
            pltpu.VMEM((per_core, srcs * CAP, width), bf16),
            pltpu.VMEM((per_core, HALVES, 2, half * CAP, width // HALVES), bf16),
            pltpu.VMEM((per_core, HALVES, half * CAP, width // HALVES), bf16),
            pltpu.VMEM((per_core, half * PACK, cols), bf16),
            pltpu.VMEM((experts * PACK, cols), bf16),
            dma((layers, per_core, 2)),
            dma((per_core, nz, nc)),
            dma((per_core, nz, nc)),
            dma((per_core, nz, nc)),
            dma((per_core, nz, nc)),
            dma((per_core, nz)),
            dma((per_core, nz)),
            dma((per_core, HALVES)),
            dma((per_core, HALVES)),
            dma((per_core, nz, nc)),
            dma((per_core, nz, nc)),
        ],
        compiler_params=pltpu.CompilerParams(
            collective_id=0, has_side_effects=True, vmem_limit_bytes=56 * 1024 * 1024
        ),
        cost_estimate=pl.CostEstimate(
            flops=flops,
            bytes_accessed=layers * per_core * width * hidden * 4,
            transcendentals=0,
        ),
    )(
        latent, time_embedding.reshape(1, width), norm_gain, jnp.swapaxes(router, 1, 2),
        jnp.swapaxes(up_proj, 2, 3), down_proj, jnp.swapaxes(routes, 2, 3),
    )
    mean_velocity = 0.5 * total
    return (latent + step_size * mean_velocity, mean_velocity)


def solution(mesh):
    placed = (
        P(("groups", "expert", "dp", "mp"), None),
        P(),
        P(),
        P(),
        P(None, "expert", None, "dp"),
        P(None, "expert", "dp", None),
        P(None, None, ("groups", "expert", "dp", "mp"), None),
    )
    return jax.shard_map(
        functools.partial(per_device, dict(mesh.shape)),
        mesh=mesh,
        in_specs=placed,
        out_specs=(
            P(("groups", "expert", "dp", "mp"), None),
            P(("groups", "expert", "dp", "mp"), None),
        ),
        check_vma=False,
    )
```
